256 devices in a mesh: rows: 16 (over z, core), cols: 16 (over x, y).
Axes of the slice: x: 4, y: 4, z: 8, core: 2. Of those that a mesh axis runs over, the one named last changes fastest.
Arguments:
- source_points: float32 [32, 32768], P(None, ('rows', 'cols')), may hold values from -3.5 to 3.5
- target_points: float32 [32, 32768], P(None, ('cols', 'rows')), may hold values from -3.5 to 3.5
- target_init: float32 [32768], P('cols'), may hold values from -3 to 3
Outputs:
- source_potential: float32 [32768], P('rows')
- target_potential: float32 [32768], P('cols')
The draws below stay inside these ranges and needn't reach their ends.
All inputs are finite; a program needn't handle non-finite values.
Results may differ from the reference program's by a relative error of at most 0.0003.
Values sent between devices are 32-bit elements; how exact they have to be, the bound alone decides.
A program may use at most 64 MiB of HBM per device.

```python
import math
import jax
import jax.numpy as jnp
from jax import lax

K = 32
ITERS = 4
NSRC = 32768
NTGT = 32768


def spread_points(key, count):
    return 0.18 * jnp.clip(jax.random.normal(key, (K, count), jnp.float32), -4.0, 4.0)


def draw_source_points(key, part):
    key = jax.random.fold_in(key, 11)
    return spread_points(key, NSRC)


def draw_target_points(key, part):
    key = jax.random.fold_in(key, 23)
    return spread_points(key, NTGT)


def steps_of(rng, extent, pieces, least, high):
    def one(dim, blocks):
        draws = jax.random.uniform(jax.random.fold_in(jax.random.fold_in(rng, 6), dim), (blocks,), jnp.float32, least / len(pieces), high / len(pieces))
        return jnp.repeat(jnp.exp(draws), extent[dim] // blocks).reshape((-1,) + (1,) * (len(extent) - dim - 1))

    gain = one(*pieces[0])
    for cut in pieces[1:]:
        gain = gain * one(*cut)
    return gain


def noise(key, shape, spread, limit, shards=(), dtype=jnp.bfloat16):
    drawn = jax.random.normal(key, shape, jnp.float32) * spread
    if len(shards) > 0:
        drawn = steps_of(key, shape, shards, -0.22, 0.18) * drawn
    return jnp.clip(drawn, min=-limit, max=limit).astype(dtype)


def setup_inputs(seed: int = 0) -> dict:
    splits = jax.random.split(jax.random.key(seed), 4)
    source_points = draw_source_points(jax.random.fold_in(splits[3], 71), 0)
    target_points = draw_target_points(jax.random.fold_in(splits[3], 71), 0)
    target_init = noise(splits[2], (NTGT,), 0.5, 3.0, ((0, 16),), jnp.float32)
    return {"source_points": source_points, "target_points": target_points, "target_init": target_init}


eps = 0.2


def cost_block(left, right):
    cross = lax.dot_general(left, right, (((0,), (0,)), ((), ())), precision=lax.Precision.HIGHEST, preferred_element_type=jnp.float32)
    sq_left = jnp.sum(left * left, axis=0)
    sq_right = jnp.sum(right * right, axis=0)
    return sq_left[:, None] + sq_right[None, :] - 2.0 * cross


def blocked(points, width):
    count = points.shape[1]
    return points.reshape(points.shape[0], count // width, width).transpose(1, 0, 2)


def reference(source_points, target_points, target_init):
    nsrc = source_points.shape[1]
    ntgt = target_points.shape[1]
    wide_src = math.gcd(nsrc, 1024)
    wide_tgt = math.gcd(ntgt, 1024)
    src_blocks = blocked(source_points, wide_src)
    tgt_blocks = blocked(target_points, wide_tgt)
    potential_g = target_init.astype(jnp.float32)
    potential_f = jnp.zeros((nsrc,), jnp.float32)
    for step in range(ITERS):
        def row_step(block):
            scores = (potential_g[None, :] - cost_block(block, target_points)) / eps
            peak = jnp.max(scores, axis=1)
            total = jnp.sum(jnp.exp(scores - peak[:, None]), axis=1)
            return eps * math.log(ntgt) - eps * (peak + jnp.log(total))

        potential_f = lax.map(row_step, src_blocks).reshape(-1)

        def col_step(block):
            scores = (potential_f[:, None] - cost_block(source_points, block)) / eps
            peak = jnp.max(scores, axis=0)
            total = jnp.sum(jnp.exp(scores - peak[None, :]), axis=0)
            return eps * math.log(nsrc) - eps * (peak + jnp.log(total))

        potential_g = lax.map(col_step, tgt_blocks).reshape(-1)
    return potential_f, potential_g
```

```python
import functools
import math

import jax
import jax.numpy as jnp
from jax import lax
from jax.experimental import pallas as pl
from jax.experimental.pallas import tpu as pltpu
from jax.sharding import PartitionSpec as P

ITERS = 4
EPS = 0.2
CHUNKS = 4
LANES = 128
ROWS_AT_ONCE = 64
DEPTH = 256
LOWEST = -1e30
TO_BITS = 1.0 / (EPS * math.log(2.0))
FROM_BITS = EPS * math.log(2.0)
MESH = pl.DeviceIdType.MESH


def ring_partners(me, size):
    steps = sorted(range(1, size), key=lambda k: -min(k // 2, (size - k) // 2))
    return [lax.rem(me + k, size) for k in steps]


def torus_partners(me, size):
    side = math.isqrt(size)
    x, y = lax.div(me, side), lax.rem(me, side)
    moves = [(a, b) for a in range(side) for b in range(side) if a + b > 0]
    moves.sort(key=lambda m: -(min(m[0], side - m[0]) + min(m[1], side - m[1])))
    return [lax.rem(x + a, side) * side + lax.rem(y + b, side) for a, b in moves]


def split3(x):
    hi = x.astype(jnp.bfloat16)
    rest = x - hi.astype(jnp.float32)
    mid = rest.astype(jnp.bfloat16)
    low = (rest - mid.astype(jnp.float32)).astype(jnp.bfloat16)
    return hi, mid, low


def send_to_all(src, dst, send_sem, recv_sem, axis, partners):
    for partner in partners:
        pltpu.make_async_remote_copy(
            src_ref=src,
            dst_ref=dst,
            send_sem=send_sem,
            recv_sem=recv_sem,
            device_id={axis: partner},
            device_id_type=MESH,
        ).start()


def wait_for_all(slots, sem):
    some = slots.at[pl.ds(0, slots.shape[0] - 1)]
    pltpu.make_async_copy(some, some, sem).wait()


def combine(parts):
    peak = jnp.max(parts, axis=0)
    return peak + jnp.log2(jnp.sum(jnp.exp2(parts - peak[None]), axis=0))


def spread(potential, wide, first):
    for q in range(potential.shape[0]):
        block = jnp.broadcast_to(potential[q : q + 1, :], (LANES, LANES))
        wide[pl.ds(pl.multiple_of(first + q * LANES, LANES), LANES), :] = block.T


def accumulate(scores, wide, first, count, lane_col, width, state):
    def step(r, state):
        rows = pl.ds(pl.multiple_of(first + r * ROWS_AT_ONCE, ROWS_AT_ONCE), ROWS_AT_ONCE)
        add = wide[rows, :]
        done = []
        for q in range(width):
            cols = pl.ds(pl.multiple_of((lane_col + q) * LANES, LANES), LANES)
            peak, total = state[q]
            z = (scores[rows, cols] + add).reshape(ROWS_AT_ONCE // 8, 8, LANES)
            top = jnp.maximum(peak, jnp.max(z, axis=0))
            total = total * jnp.exp2(peak - top) + jnp.sum(jnp.exp2(z - top[None]), axis=0)
            done.append((top, total))
        return tuple(done)

    steps = count // ROWS_AT_ONCE
    return lax.fori_loop(0, steps, step, state, unroll=min(8, steps))


def fresh(width):
    low = jnp.full((8, LANES), LOWEST, jnp.float32)
    return ((low, jnp.zeros((8, LANES), jnp.float32)),) * width


def finish(peak, total):
    top = jnp.max(peak, axis=0, keepdims=True)
    return top + jnp.log2(jnp.sum(total * jnp.exp2(peak - top), axis=0, keepdims=True))


def kernel(
    nr, nc, s_ref, t_ref, g_ref, f_out, g_out,
    s_all, t_all, s_cat, t_cat, s_rows, t_rows, w, wt, p_wide, q_wide, p_now, s_sq, t_sq, peaks, totals, p_parts, q_parts,
    pt_send, pt_recv, p_send, p_recv, q_send, q_recv,
):
    row, col = lax.axis_index("rows"), lax.axis_index("cols")
    in_rows = ring_partners(row, nr)
    in_cols = torus_partners(col, nc)
    n_src, n_tgt = nc * LANES, nr * LANES
    src_width, tgt_width = nc // CHUNKS, nr // CHUNKS
    bits_src = math.log2(n_src * nr)
    bits_tgt = math.log2(n_tgt * nc)

    barrier = pltpu.get_barrier_semaphore()
    for axis, partners in (("rows", in_rows), ("cols", in_cols)):
        for partner in partners:
            pl.semaphore_signal(barrier, inc=1, device_id={axis: partner}, device_id_type=MESH)
    pl.semaphore_wait(barrier, len(in_rows) + len(in_cols))

    send_to_all(t_ref, t_all.at[row], pt_send.at[0], pt_recv.at[0], "rows", in_rows)
    send_to_all(s_ref, s_all.at[col], pt_send.at[1], pt_recv.at[1], "cols", in_cols)
    t_all[row] = t_ref[...]
    s_all[col] = s_ref[...]
    empty = jnp.zeros((DEPTH - 6 * 32, LANES), jnp.bfloat16)

    def lay(points, scale, order, cat, turned, sq, q):
        x = points[q]
        sq[pl.ds(q, 1), :] = jnp.sum(x * x, axis=0, keepdims=True)
        pieces = split3(x * scale)
        block = jnp.concatenate([pieces[k] for k in order] + [empty], axis=0)
        at = pl.ds(pl.multiple_of(q * LANES, LANES), LANES)
        cat[:, at] = block
        turned[at, :] = block.T

    wait_for_all(s_all, pt_recv.at[1])

    @pl.loop(0, nc)
    def _(q):
        lay(s_all, 1.0, (0, 0, 1, 1, 0, 2), s_cat, s_rows, s_sq, q)

    wait_for_all(t_all, pt_recv.at[0])

    @pl.loop(0, nr)
    def _(q):
        lay(t_all, 2.0 * TO_BITS, (0, 1, 0, 1, 2, 0), t_cat, t_rows, t_sq, q)

    def products(left, right, out):
        @pl.loop(0, left.shape[0] // 256)
        def _(b):
            at = pl.ds(pl.multiple_of(b * 256, 256), 256)
            for c in range(right.shape[1] // 256):
                cols = pl.ds(c * 256, 256)
                out[at, cols] = jnp.dot(left[at, :], right[:, cols], preferred_element_type=jnp.float32)

    products(t_rows, s_cat, wt)
    products(s_rows, t_cat, w)
    spread((g_ref[...] - t_sq[...]) * TO_BITS, q_wide, 0)
    wait_for_all(t_all, pt_send.at[0])
    wait_for_all(s_all, pt_send.at[1])

    @pl.loop(0, ITERS)
    def _(it):
        @pl.loop(0, CHUNKS)
        def _(c):
            state = accumulate(wt, q_wide, 0, n_tgt, c * src_width, src_width, fresh(src_width))
            for q in range(src_width):
                p_parts[it, c, col, q : q + 1, :] = finish(*state[q])
            here = p_parts.at[it, c, col]
            send_to_all(here, here, p_send.at[it, c], p_recv.at[it, c], "cols", in_cols)

        @pl.loop(0, CHUNKS)
        def _(c):
            for q in range(tgt_width):
                peaks[c, q] = jnp.full((8, LANES), LOWEST, jnp.float32)
                totals[c, q] = jnp.zeros((8, LANES), jnp.float32)

        @pl.loop(0, CHUNKS)
        def _(c):
            wait_for_all(p_parts.at[it, c], p_send.at[it, c])
            wait_for_all(p_parts.at[it, c], p_recv.at[it, c])
            p = bits_tgt - combine(p_parts[it, c])
            p_now[c] = p
            depth = src_width * LANES
            spread(p, p_wide, c * depth)

            @pl.loop(0, CHUNKS)
            def _(d):
                state = tuple((peaks[d, q], totals[d, q]) for q in range(tgt_width))
                state = accumulate(w, p_wide, c * depth, depth, d * tgt_width, tgt_width, state)
                for q in range(tgt_width):
                    peaks[d, q], totals[d, q] = state[q]

                @pl.when(c == CHUNKS - 1)
                def _():
                    for q in range(tgt_width):
                        q_parts[it, d, row, q : q + 1, :] = finish(*state[q])
                    here = q_parts.at[it, d, row]
                    send_to_all(here, here, q_send.at[it, d], q_recv.at[it, d], "rows", in_rows)

        @pl.loop(0, CHUNKS)
        def _(d):
            wait_for_all(q_parts.at[it, d], q_send.at[it, d])
            wait_for_all(q_parts.at[it, d], q_recv.at[it, d])
            spread(bits_src - combine(q_parts[it, d]), q_wide, d * tgt_width * LANES)

    for c in range(CHUNKS):
        at = slice(c * src_width, (c + 1) * src_width)
        f_out[at, :] = s_sq[at, :] + FROM_BITS * p_now[c]
        at = slice(c * tgt_width, (c + 1) * tgt_width)
        g_out[at, :] = t_sq[at, :] + FROM_BITS * (bits_src - combine(q_parts[ITERS - 1, c]))


def body(source_points, target_points, target_init):
    nr, nc = lax.axis_size("rows"), lax.axis_size("cols")
    n_src, n_tgt = nc * LANES, nr * LANES
    f32, bf16 = jnp.float32, jnp.bfloat16
    src_width, tgt_width = nc // CHUNKS, nr // CHUNKS
    f, g = pl.pallas_call(
        functools.partial(kernel, nr, nc),
        out_shape=(jax.ShapeDtypeStruct((nc, LANES), f32), jax.ShapeDtypeStruct((nr, LANES), f32)),
        in_specs=[pl.BlockSpec(memory_space=pltpu.VMEM)] * 3,
        out_specs=[pl.BlockSpec(memory_space=pltpu.VMEM)] * 2,
        scratch_shapes=[
            pltpu.VMEM((nc,) + source_points.shape, f32),
            pltpu.VMEM((nr,) + target_points.shape, f32),
            pltpu.VMEM((DEPTH, n_src), bf16),
            pltpu.VMEM((DEPTH, n_tgt), bf16),
            pltpu.VMEM((n_src, DEPTH), bf16),
            pltpu.VMEM((n_tgt, DEPTH), bf16),
            pltpu.VMEM((n_src, n_tgt), f32),
            pltpu.VMEM((n_tgt, n_src), f32),
            pltpu.VMEM((n_src, LANES), f32),
            pltpu.VMEM((n_tgt, LANES), f32),
            pltpu.VMEM((CHUNKS, src_width, LANES), f32),
            pltpu.VMEM((nc, LANES), f32),
            pltpu.VMEM((nr, LANES), f32),
            pltpu.VMEM((CHUNKS, tgt_width, 8, LANES), f32),
            pltpu.VMEM((CHUNKS, tgt_width, 8, LANES), f32),
            pltpu.VMEM((ITERS, CHUNKS, nc, src_width, LANES), f32),
            pltpu.VMEM((ITERS, CHUNKS, nr, tgt_width, LANES), f32),
            pltpu.SemaphoreType.DMA((2,)),
            pltpu.SemaphoreType.DMA((2,)),
            pltpu.SemaphoreType.DMA((ITERS, CHUNKS)),
            pltpu.SemaphoreType.DMA((ITERS, CHUNKS)),
            pltpu.SemaphoreType.DMA((ITERS, CHUNKS)),
            pltpu.SemaphoreType.DMA((ITERS, CHUNKS)),
        ],
        compiler_params=pltpu.CompilerParams(
            collective_id=0, has_side_effects=True, vmem_limit_bytes=56 << 20
        ),
        name="sinkhorn",
    )(source_points, target_points, target_init.reshape(nr, LANES))
    return f.reshape(-1), g.reshape(-1)


def solution(mesh):
    in_specs = (P(None, ("rows", "cols")), P(None, ("cols", "rows")), P("cols"))
    out_specs = (P("rows"), P("cols"))
    return jax.shard_map(body, mesh=mesh, in_specs=in_specs, out_specs=out_specs, check_vma=False)
```

```python
import functools
import math

import jax
import jax.numpy as jnp
from jax import lax
from jax.experimental import pallas as pl
from jax.experimental.pallas import tpu as pltpu
from jax.sharding import PartitionSpec as P

ITERS = 4
EPS = 0.2
SRC_CUTS = (8, 8)
TGT_CUTS = (8, 8)
LANES = 128
ROWS_AT_ONCE = 64
DEPTH = 256
LOWEST = -1e30
TO_BITS = 1.0 / (EPS * math.log(2.0))
FROM_BITS = EPS * math.log(2.0)
MESH = pl.DeviceIdType.MESH


def ring_partners(me, size):
    steps = sorted(range(1, size), key=lambda k: -min(k // 2, (size - k) // 2))
    return [lax.rem(me + k, size) for k in steps]


def torus_partners(me, size):
    side = math.isqrt(size)
    x, y = lax.div(me, side), lax.rem(me, side)
    moves = [(a, b) for a in range(side) for b in range(side) if a + b > 0]
    moves.sort(key=lambda m: -(min(m[0], side - m[0]) + min(m[1], side - m[1])))
    return [lax.rem(x + a, side) * side + lax.rem(y + b, side) for a, b in moves]


def split3(x):
    hi = x.astype(jnp.bfloat16)
    rest = x - hi.astype(jnp.float32)
    mid = rest.astype(jnp.bfloat16)
    low = (rest - mid.astype(jnp.float32)).astype(jnp.bfloat16)
    return hi, mid, low


def send_to_all(src, dst, send_sem, recv_sem, axis, partners):
    for partner in partners:
        pltpu.make_async_remote_copy(
            src_ref=src,
            dst_ref=dst,
            send_sem=send_sem,
            recv_sem=recv_sem,
            device_id={axis: partner},
            device_id_type=MESH,
        ).start()


def wait_for_all(slots, sem):
    some = slots.at[pl.ds(0, slots.shape[0] - 1)]
    pltpu.make_async_copy(some, some, sem).wait()


def combine(parts):
    peak = jnp.max(parts, axis=0)
    return peak + jnp.log2(jnp.sum(jnp.exp2(parts - peak[None]), axis=0))


def spread(potential, wide, first):
    for q in range(potential.shape[0]):
        block = jnp.broadcast_to(potential[q : q + 1, :], (LANES, LANES))
        wide[pl.ds(pl.multiple_of(first + q * LANES, LANES), LANES), :] = block.T


def accumulate(scores, wide, first, count, lane_col, width, state):
    def step(r, state):
        rows = pl.ds(pl.multiple_of(first + r * ROWS_AT_ONCE, ROWS_AT_ONCE), ROWS_AT_ONCE)
        add = wide[rows, :]
        done = []
        for q in range(width):
            cols = pl.ds((lane_col + q) * LANES, LANES)
            peak, total = state[q]
            z = (scores[rows, cols] + add).reshape(ROWS_AT_ONCE // 8, 8, LANES)
            top = jnp.maximum(peak, jnp.max(z, axis=0))
            total = total * jnp.exp2(peak - top) + jnp.sum(jnp.exp2(z - top[None]), axis=0)
            done.append((top, total))
        return tuple(done)

    steps = count // ROWS_AT_ONCE
    return lax.fori_loop(0, steps, step, state, unroll=min(max(8, 64 // width), steps))


def fresh(width):
    low = jnp.full((8, LANES), LOWEST, jnp.float32)
    return ((low, jnp.zeros((8, LANES), jnp.float32)),) * width


def finish(peak, total):
    top = jnp.max(peak, axis=0, keepdims=True)
    return top + jnp.log2(jnp.sum(total * jnp.exp2(peak - top), axis=0, keepdims=True))


def cut(cuts, blocks):
    unit = blocks // sum(cuts) if blocks >= sum(cuts) else 0
    widths = [c * unit for c in cuts] if unit else [blocks // 2, blocks // 2]
    return [(sum(widths[:k]), width) for k, width in enumerate(widths)]


def kernel(nr, nc, s_in, t_in, g_in, f_out, g_out, *scratch):
    scratch = list(scratch)
    s_all, t_all, s_cat, t_cat, s_rows, t_rows, w, wt, p_wide, q_wide, s_sq, t_sq, g_now, p_now = scratch[:14]
    local, s_sem, t_send, t_recv, p_sem, q_sem = scratch[14:20]
    src_chunks, tgt_chunks = cut(SRC_CUTS, nc), cut(TGT_CUTS, nr)
    p_parts = scratch[20 : 20 + len(src_chunks)]
    q_parts = scratch[20 + len(src_chunks) :]
    row, col = lax.axis_index("rows"), lax.axis_index("cols")
    in_rows = ring_partners(row, nr)
    in_cols = torus_partners(col, nc)
    n_src, n_tgt = nc * LANES, nr * LANES
    bits_src = math.log2(n_src * nr)
    bits_tgt = math.log2(n_tgt * nc)

    barrier = pltpu.get_barrier_semaphore()
    for axis, partners in (("rows", in_rows), ("cols", in_cols)):
        for partner in partners:
            pl.semaphore_signal(barrier, inc=1, device_id={axis: partner}, device_id_type=MESH)
    staged = [
        pltpu.make_async_copy(t_in, t_all.at[row], local.at[0]),
        pltpu.make_async_copy(s_in, s_all.at[col], local.at[1]),
        pltpu.make_async_copy(g_in, g_now, local.at[2]),
    ]
    for copy in staged:
        copy.start()
    for copy in staged:
        copy.wait()
    pl.semaphore_wait(barrier, len(in_rows) + len(in_cols))

    core = lax.rem(row, 2)
    sibling = row + 1 - 2 * core
    chips = nr // 2

    def far_row(step):
        return lax.rem(row + 2 * step, nr)

    def target_copy(shard, to, send_sem):
        return pltpu.make_async_remote_copy(
            src_ref=t_all.at[shard],
            dst_ref=t_all.at[shard],
            send_sem=send_sem,
            recv_sem=t_recv.at[shard],
            device_id={"rows": to},
            device_id_type=MESH,
        )

    by_distance = sorted(range(1, chips), key=lambda k: min(k, chips - k))
    for step in reversed(by_distance):
        target_copy(row, far_row(step), t_send.at[0]).start()
    here = s_all.at[col]
    send_to_all(here, here, s_sem.at[0], s_sem.at[1], "cols", in_cols)
    target_copy(row, sibling, t_send.at[1]).start()
    for step in by_distance:
        shard = far_row(step)
        target_copy(shard, sibling, t_send.at[1]).wait_recv()
        target_copy(shard, sibling, t_send.at[1]).start()
    empty = jnp.zeros((DEPTH - 6 * 32, LANES), jnp.bfloat16)

    def lay(points, scale, order, cat, turned, sq, q):
        x = points[q]
        sq[pl.ds(q, 1), :] = jnp.sum(x * x, axis=0, keepdims=True)
        pieces = split3(x * scale)
        block = jnp.concatenate([pieces[k] for k in order] + [empty], axis=0)
        at = pl.ds(pl.multiple_of(q * LANES, LANES), LANES)
        cat[:, at] = block
        turned[at, :] = block.T

    wait_for_all(s_all, s_sem.at[1])

    @pl.loop(0, nc)
    def _(q):
        lay(s_all, 1.0, (0, 0, 1, 1, 0, 2), s_cat, s_rows, s_sq, q)

    for step in [0] + by_distance:
        shard = far_row(step) + 1 - 2 * core
        target_copy(shard, sibling, t_send.at[1]).wait_recv()

    @pl.loop(0, nr)
    def _(q):
        lay(t_all, 2.0 * TO_BITS, (0, 1, 0, 1, 2, 0), t_cat, t_rows, t_sq, q)

    def products(left, right, out):
        tile = min(512, right.shape[1])

        @pl.loop(0, right.shape[1] // tile)
        def _(c):
            cols = pl.ds(pl.multiple_of(c * tile, tile), tile)
            out[:, cols] = jnp.dot(left[...], right[:, cols], preferred_element_type=jnp.float32)

    products(t_rows, s_cat, wt)
    spread((g_now[...] - t_sq[...]) * TO_BITS, q_wide, 0)

    @pl.loop(0, ITERS)
    def _(it):
        for c, (first, width) in enumerate(src_chunks):
            state = accumulate(wt, q_wide, 0, n_tgt, first, width, fresh(width))
            for q in range(width):
                p_parts[c][it, col, q : q + 1, :] = finish(*state[q])
            here = p_parts[c].at[it, col]
            send_to_all(here, here, p_sem.at[0, it, c], p_sem.at[1, it, c], "cols", in_cols)

        @pl.when(it == 0)
        def _():
            products(s_rows, t_cat, w)
            wait_for_all(s_all, s_sem.at[0])
            some = t_all.at[pl.ds(0, chips - 1)]
            pltpu.make_async_copy(some, some, t_send.at[0]).wait()
            some = t_all.at[pl.ds(0, chips)]
            pltpu.make_async_copy(some, some, t_send.at[1]).wait()

        whole = fresh(nr)
        for c, (first, width) in enumerate(src_chunks):
            wait_for_all(p_parts[c].at[it], p_sem.at[0, it, c])
            wait_for_all(p_parts[c].at[it], p_sem.at[1, it, c])
            p = bits_tgt - combine(p_parts[c][it])
            p_now[first : first + width, :] = p
            start, depth = first * LANES, width * LANES
            spread(p, p_wide, start)
            if c < len(src_chunks) - 1:
                whole = accumulate(w, p_wide, start, depth, 0, nr, whole)
                continue
            for d, (lane_col, cols) in enumerate(tgt_chunks):
                state = accumulate(w, p_wide, start, depth, lane_col, cols, whole[lane_col : lane_col + cols])
                for q in range(cols):
                    q_parts[d][it, row, q : q + 1, :] = finish(*state[q])
                here = q_parts[d].at[it, row]
                send_to_all(here, here, q_sem.at[0, it, d], q_sem.at[1, it, d], "rows", in_rows)

        for d, (first, width) in enumerate(tgt_chunks):
            wait_for_all(q_parts[d].at[it], q_sem.at[0, it, d])
            wait_for_all(q_parts[d].at[it], q_sem.at[1, it, d])
            q = bits_src - combine(q_parts[d][it])
            g_now[first : first + width, :] = q
            spread(q, q_wide, first * LANES)

    f_out[...] = s_sq[...] + FROM_BITS * p_now[...]
    g_out[...] = t_sq[...] + FROM_BITS * g_now[...]


def body(source_points, target_points, target_init):
    nr, nc = lax.axis_size("rows"), lax.axis_size("cols")
    n_src, n_tgt = nc * LANES, nr * LANES
    f32, bf16 = jnp.float32, jnp.bfloat16
    src_chunks, tgt_chunks = cut(SRC_CUTS, nc), cut(TGT_CUTS, nr)
    f, g = pl.pallas_call(
        functools.partial(kernel, nr, nc),
        out_shape=(jax.ShapeDtypeStruct((nc, LANES), f32), jax.ShapeDtypeStruct((nr, LANES), f32)),
        in_specs=[pl.BlockSpec(memory_space=pl.ANY)] * 3,
        out_specs=[pl.BlockSpec(memory_space=pltpu.VMEM)] * 2,
        scratch_shapes=[
            pltpu.VMEM((nc,) + source_points.shape, f32),
            pltpu.VMEM((nr,) + target_points.shape, f32),
            pltpu.VMEM((DEPTH, n_src), bf16),
            pltpu.VMEM((DEPTH, n_tgt), bf16),
            pltpu.VMEM((n_src, DEPTH), bf16),
            pltpu.VMEM((n_tgt, DEPTH), bf16),
            pltpu.VMEM((n_src, n_tgt), f32),
            pltpu.VMEM((n_tgt, n_src), f32),
            pltpu.VMEM((n_src, LANES), f32),
            pltpu.VMEM((n_tgt, LANES), f32),
            pltpu.VMEM((nc, LANES), f32),
            pltpu.VMEM((nr, LANES), f32),
            pltpu.VMEM((nr, LANES), f32),
            pltpu.VMEM((nc, LANES), f32),
            pltpu.SemaphoreType.DMA((3,)),
            pltpu.SemaphoreType.DMA((2,)),
            pltpu.SemaphoreType.DMA((2,)),
            pltpu.SemaphoreType.DMA((nr,)),
            pltpu.SemaphoreType.DMA((2, ITERS, len(src_chunks))),
            pltpu.SemaphoreType.DMA((2, ITERS, len(tgt_chunks))),
        ]
        + [pltpu.VMEM((ITERS, nc, width, LANES), f32) for _, width in src_chunks]
        + [pltpu.VMEM((ITERS, nr, width, LANES), f32) for _, width in tgt_chunks],
        compiler_params=pltpu.CompilerParams(
            collective_id=0, has_side_effects=True, vmem_limit_bytes=56 << 20
        ),
        name="sinkhorn",
    )(source_points, target_points, target_init.reshape(nr, LANES))
    return f.reshape(-1), g.reshape(-1)


def solution(mesh):
    in_specs = (P(None, ("rows", "cols")), P(None, ("cols", "rows")), P("cols"))
    out_specs = (P("rows"), P("cols"))
    return jax.shard_map(body, mesh=mesh, in_specs=in_specs, out_specs=out_specs, check_vma=False)
```

```python
import functools
import math

import jax
import jax.numpy as jnp
from jax import lax
from jax.experimental import pallas as pl
from jax.experimental.pallas import tpu as pltpu
from jax.sharding import PartitionSpec as P

ITERS = 4
EPS = 0.2
SRC_CUTS = (8, 8)
TGT_CUTS = (8, 8)
LANES = 128
ROWS_AT_ONCE = 64
DEPTH = 256
LOWEST = -1e30
TO_BITS = 1.0 / (EPS * math.log(2.0))
FROM_BITS = EPS * math.log(2.0)
MESH = pl.DeviceIdType.MESH


def ring_partners(me, size):
    steps = sorted(range(1, size), key=lambda k: -min(k // 2, (size - k) // 2))
    return [lax.rem(me + k, size) for k in steps]


def torus_partners(me, size):
    side = math.isqrt(size)
    x, y = lax.div(me, side), lax.rem(me, side)
    moves = [(a, b) for a in range(side) for b in range(side) if a + b > 0]
    moves.sort(key=lambda m: -(min(m[0], side - m[0]) + min(m[1], side - m[1])))
    return [lax.rem(x + a, side) * side + lax.rem(y + b, side) for a, b in moves]


def split3(x):
    hi = x.astype(jnp.bfloat16)
    rest = x - hi.astype(jnp.float32)
    mid = rest.astype(jnp.bfloat16)
    low = (rest - mid.astype(jnp.float32)).astype(jnp.bfloat16)
    return hi, mid, low


def send_to_all(src, dst, send_sem, recv_sem, axis, partners):
    for partner in partners:
        pltpu.make_async_remote_copy(
            src_ref=src,
            dst_ref=dst,
            send_sem=send_sem,
            recv_sem=recv_sem,
            device_id={axis: partner},
            device_id_type=MESH,
        ).start()


def wait_for_all(slots, sem):
    some = slots.at[pl.ds(0, slots.shape[0] - 1)]
    pltpu.make_async_copy(some, some, sem).wait()


def combine(parts):
    peak = jnp.max(parts, axis=0)
    return peak + jnp.log2(jnp.sum(jnp.exp2(parts - peak[None]), axis=0))


def spread(potential, wide, first):
    for q in range(potential.shape[0]):
        block = jnp.broadcast_to(potential[q : q + 1, :], (LANES, LANES))
        wide[pl.ds(pl.multiple_of(first + q * LANES, LANES), LANES), :] = block.T


def accumulate(scores, wide, first, count, lane_col, width, state):
    def step(r, state):
        rows = pl.ds(pl.multiple_of(first + r * ROWS_AT_ONCE, ROWS_AT_ONCE), ROWS_AT_ONCE)
        add = wide[rows, :]
        done = []
        for q in range(width):
            cols = pl.ds((lane_col + q) * LANES, LANES)
            peak, total = state[q]
            z = (scores[rows, cols] + add).reshape(ROWS_AT_ONCE // 8, 8, LANES)
            top = jnp.maximum(peak, jnp.max(z, axis=0))
            total = total * jnp.exp2(peak - top) + jnp.sum(jnp.exp2(z - top[None]), axis=0)
            done.append((top, total))
        return tuple(done)

    steps = count // ROWS_AT_ONCE
    return lax.fori_loop(0, steps, step, state, unroll=min(max(8, 64 // width), steps))


def fresh(width):
    low = jnp.full((8, LANES), LOWEST, jnp.float32)
    return ((low, jnp.zeros((8, LANES), jnp.float32)),) * width


def finish(peak, total):
    top = jnp.max(peak, axis=0, keepdims=True)
    return top + jnp.log2(jnp.sum(total * jnp.exp2(peak - top), axis=0, keepdims=True))


def cut(cuts, blocks):
    unit = blocks // sum(cuts) if blocks >= sum(cuts) else 0
    widths = [c * unit for c in cuts] if unit else [blocks // 2, blocks // 2]
    return [(sum(widths[:k]), width) for k, width in enumerate(widths)]


def kernel(nr, nc, s_in, t_in, g_in, f_out, g_out, *scratch):
    scratch = list(scratch)
    s_all, t_all, s_cat, t_cat, s_rows, t_rows, w, wt, p_wide, q_wide, s_sq, t_sq, g_now, p_now = scratch[:14]
    local, s_sem, t_send, t_recv, p_sem, q_sem = scratch[14:20]
    src_chunks, tgt_chunks = cut(SRC_CUTS, nc), cut(TGT_CUTS, nr)
    p_parts = scratch[20 : 20 + len(src_chunks)]
    q_parts = scratch[20 + len(src_chunks) :]
    row, col = lax.axis_index("rows"), lax.axis_index("cols")
    in_rows = ring_partners(row, nr)
    in_cols = torus_partners(col, nc)
    n_src, n_tgt = nc * LANES, nr * LANES
    bits_src = math.log2(n_src * nr)
    bits_tgt = math.log2(n_tgt * nc)

    barrier = pltpu.get_barrier_semaphore()
    for axis, partners in (("rows", in_rows), ("cols", in_cols)):
        for partner in partners:
            pl.semaphore_signal(barrier, inc=1, device_id={axis: partner}, device_id_type=MESH)
    staged = [
        pltpu.make_async_copy(t_in, t_all.at[row], local.at[0]),
        pltpu.make_async_copy(s_in, s_all.at[col], local.at[1]),
        pltpu.make_async_copy(g_in, g_now, local.at[2]),
    ]
    for copy in staged:
        copy.start()
    for copy in staged:
        copy.wait()
    pl.semaphore_wait(barrier, len(in_rows) + len(in_cols))

    core = lax.rem(row, 2)
    sibling = row + 1 - 2 * core
    chips = nr // 2

    def far_row(step):
        return lax.rem(row + 2 * step, nr)

    def target_copy(shard, to, send_sem):
        return pltpu.make_async_remote_copy(
            src_ref=t_all.at[shard],
            dst_ref=t_all.at[shard],
            send_sem=send_sem,
            recv_sem=t_recv.at[shard],
            device_id={"rows": to},
            device_id_type=MESH,
        )

    by_distance = sorted(range(1, chips), key=lambda k: min(k, chips - k))
    for step in reversed(by_distance):
        target_copy(row, far_row(step), t_send.at[0]).start()
    here = s_all.at[col]
    send_to_all(here, here, s_sem.at[0], s_sem.at[1], "cols", in_cols)
    target_copy(row, sibling, t_send.at[1]).start()
    for step in by_distance:
        shard = far_row(step)
        target_copy(shard, sibling, t_send.at[1]).wait_recv()
        target_copy(shard, sibling, t_send.at[1]).start()
    empty = jnp.zeros((DEPTH - 6 * 32, LANES), jnp.bfloat16)

    def lay(points, scale, order, cat, turned, sq, q):
        x = points[q]
        sq[pl.ds(q, 1), :] = jnp.sum(x * x, axis=0, keepdims=True)
        pieces = split3(x * scale)
        block = jnp.concatenate([pieces[k] for k in order] + [empty], axis=0)
        at = pl.ds(pl.multiple_of(q * LANES, LANES), LANES)
        cat[:, at] = block
        turned[at, :] = block.T

    wait_for_all(s_all, s_sem.at[1])

    @pl.loop(0, nc)
    def _(q):
        lay(s_all, 1.0, (0, 0, 1, 1, 0, 2), s_cat, s_rows, s_sq, q)

    def lay_target(shard):
        lay(t_all, 2.0 * TO_BITS, (0, 1, 0, 1, 2, 0), t_cat, t_rows, t_sq, shard)
        start = (g_now[pl.ds(shard, 1), :] - t_sq[pl.ds(shard, 1), :]) * TO_BITS
        spread(start, q_wide, shard * LANES)

    def nearest(k):
        away = lax.div(k + 1, 2)
        return lax.rem(row + 2 * (chips + (2 * lax.rem(k, 2) - 1) * away), nr)

    @pl.loop(0, chips)
    def _(k):
        lay_target(nearest(k))

    @pl.loop(0, chips)
    def _(k):
        shard = nearest(k) + 1 - 2 * core
        target_copy(shard, sibling, t_send.at[1]).wait_recv()
        lay_target(shard)

    def products(left, right, out):
        tile = min(512, right.shape[1])

        @pl.loop(0, right.shape[1] // tile)
        def _(c):
            cols = pl.ds(pl.multiple_of(c * tile, tile), tile)
            out[:, cols] = jnp.dot(left[...], right[:, cols], preferred_element_type=jnp.float32)

    products(t_rows, s_cat, wt)

    def take_target(it, d):
        first, width = tgt_chunks[d]
        wait_for_all(q_parts[d].at[it], q_sem.at[0, it, d])
        wait_for_all(q_parts[d].at[it], q_sem.at[1, it, d])
        q = bits_src - combine(q_parts[d][it])
        g_now[first : first + width, :] = q
        return q

    @pl.loop(0, ITERS)
    def _(it):
        for c, (first, width) in enumerate(src_chunks):
            state = fresh(width)
            if c == 0:
                for d, (lane_col, cols) in enumerate(tgt_chunks):

                    @pl.when(it > 0)
                    def _():
                        spread(take_target(it - 1, d), q_wide, lane_col * LANES)

                    state = accumulate(wt, q_wide, lane_col * LANES, cols * LANES, first, width, state)
            else:
                state = accumulate(wt, q_wide, 0, n_tgt, first, width, state)
            for q in range(width):
                p_parts[c][it, col, q : q + 1, :] = finish(*state[q])
            here = p_parts[c].at[it, col]
            send_to_all(here, here, p_sem.at[0, it, c], p_sem.at[1, it, c], "cols", in_cols)

        @pl.when(it == 0)
        def _():
            products(s_rows, t_cat, w)
            wait_for_all(s_all, s_sem.at[0])
            some = t_all.at[pl.ds(0, chips - 1)]
            pltpu.make_async_copy(some, some, t_send.at[0]).wait()
            some = t_all.at[pl.ds(0, chips)]
            pltpu.make_async_copy(some, some, t_send.at[1]).wait()

        whole = fresh(nr)
        for c, (first, width) in enumerate(src_chunks):
            wait_for_all(p_parts[c].at[it], p_sem.at[0, it, c])
            wait_for_all(p_parts[c].at[it], p_sem.at[1, it, c])
            p = bits_tgt - combine(p_parts[c][it])
            p_now[first : first + width, :] = p
            start, depth = first * LANES, width * LANES
            spread(p, p_wide, start)
            if c < len(src_chunks) - 1:
                whole = accumulate(w, p_wide, start, depth, 0, nr, whole)
                continue
            for d, (lane_col, cols) in enumerate(tgt_chunks):
                state = accumulate(w, p_wide, start, depth, lane_col, cols, whole[lane_col : lane_col + cols])
                for q in range(cols):
                    q_parts[d][it, row, q : q + 1, :] = finish(*state[q])
                here = q_parts[d].at[it, row]
                send_to_all(here, here, q_sem.at[0, it, d], q_sem.at[1, it, d], "rows", in_rows)

    for d in range(len(tgt_chunks)):
        take_target(ITERS - 1, d)
    f_out[...] = s_sq[...] + FROM_BITS * p_now[...]
    g_out[...] = t_sq[...] + FROM_BITS * g_now[...]


def hand_over(f_ref, g_ref, f_out, g_out):
    f_out[...] = f_ref[...]
    g_out[...] = g_ref[...]


def body(source_points, target_points, target_init):
    nr, nc = lax.axis_size("rows"), lax.axis_size("cols")
    n_src, n_tgt = nc * LANES, nr * LANES
    f32, bf16 = jnp.float32, jnp.bfloat16
    src_chunks, tgt_chunks = cut(SRC_CUTS, nc), cut(TGT_CUTS, nr)
    f, g = pl.pallas_call(
        functools.partial(kernel, nr, nc),
        out_shape=(jax.ShapeDtypeStruct((nc, LANES), f32), jax.ShapeDtypeStruct((nr, LANES), f32)),
        in_specs=[pl.BlockSpec(memory_space=pl.ANY)] * 3,
        out_specs=[pl.BlockSpec(memory_space=pltpu.VMEM)] * 2,
        scratch_shapes=[
            pltpu.VMEM((nc,) + source_points.shape, f32),
            pltpu.VMEM((nr,) + target_points.shape, f32),
            pltpu.VMEM((DEPTH, n_src), bf16),
            pltpu.VMEM((DEPTH, n_tgt), bf16),
            pltpu.VMEM((n_src, DEPTH), bf16),
            pltpu.VMEM((n_tgt, DEPTH), bf16),
            pltpu.VMEM((n_src, n_tgt), f32),
            pltpu.VMEM((n_tgt, n_src), f32),
            pltpu.VMEM((n_src, LANES), f32),
            pltpu.VMEM((n_tgt, LANES), f32),
            pltpu.VMEM((nc, LANES), f32),
            pltpu.VMEM((nr, LANES), f32),
            pltpu.VMEM((nr, LANES), f32),
            pltpu.VMEM((nc, LANES), f32),
            pltpu.SemaphoreType.DMA((3,)),
            pltpu.SemaphoreType.DMA((2,)),
            pltpu.SemaphoreType.DMA((2,)),
            pltpu.SemaphoreType.DMA((nr,)),
            pltpu.SemaphoreType.DMA((2, ITERS, len(src_chunks))),
            pltpu.SemaphoreType.DMA((2, ITERS, len(tgt_chunks))),
        ]
        + [pltpu.VMEM((ITERS, nc, width, LANES), f32) for _, width in src_chunks]
        + [pltpu.VMEM((ITERS, nr, width, LANES), f32) for _, width in tgt_chunks],
        compiler_params=pltpu.CompilerParams(
            collective_id=0, has_side_effects=True, vmem_limit_bytes=56 << 20
        ),
        name="sinkhorn",
    )(source_points, target_points, target_init.reshape(nr, LANES))
    f, g = pl.pallas_call(
        hand_over,
        out_shape=(jax.ShapeDtypeStruct((nc, LANES), f32), jax.ShapeDtypeStruct((nr, LANES), f32)),
        in_specs=[pl.BlockSpec(memory_space=pltpu.VMEM)] * 2,
        out_specs=[pl.BlockSpec(memory_space=pltpu.VMEM)] * 2,
        name="hand_over",
    )(f, g)
    return f.reshape(-1), g.reshape(-1)


def solution(mesh):
    in_specs = (P(None, ("rows", "cols")), P(None, ("cols", "rows")), P("cols"))
    out_specs = (P("rows"), P("cols"))
    return jax.shard_map(body, mesh=mesh, in_specs=in_specs, out_specs=out_specs, check_vma=False)
```

```python
import functools
import math

import jax
import jax.numpy as jnp
from jax import lax
from jax.experimental import pallas as pl
from jax.experimental.pallas import tpu as pltpu
from jax.sharding import PartitionSpec as P

ITERS = 4
EPS = 0.2
SRC_CUTS = (8, 8)
TGT_CUTS = (8, 8)
LANES = 128
ROWS_AT_ONCE = 64
DEPTH = 256
LOWEST = -1e30
TO_BITS = 1.0 / (EPS * math.log(2.0))
FROM_BITS = EPS * math.log(2.0)
MESH = pl.DeviceIdType.MESH


def ring_partners(me, size):
    steps = sorted(range(1, size), key=lambda k: -min(k // 2, (size - k) // 2))
    return [lax.rem(me + k, size) for k in steps]


def torus_partners(me, size):
    side = math.isqrt(size)
    x, y = lax.div(me, side), lax.rem(me, side)
    moves = [(a, b) for a in range(side) for b in range(side) if a + b > 0]
    moves.sort(key=lambda m: -(min(m[0], side - m[0]) + min(m[1], side - m[1])))
    return [lax.rem(x + a, side) * side + lax.rem(y + b, side) for a, b in moves]


def split3(x):
    hi = x.astype(jnp.bfloat16)
    rest = x - hi.astype(jnp.float32)
    mid = rest.astype(jnp.bfloat16)
    low = (rest - mid.astype(jnp.float32)).astype(jnp.bfloat16)
    return hi, mid, low


def send_to_all(src, dst, send_sem, recv_sem, axis, partners):
    for partner in partners:
        pltpu.make_async_remote_copy(
            src_ref=src,
            dst_ref=dst,
            send_sem=send_sem,
            recv_sem=recv_sem,
            device_id={axis: partner},
            device_id_type=MESH,
        ).start()


def wait_for_all(slots, sem):
    some = slots.at[pl.ds(0, slots.shape[0] - 1)]
    pltpu.make_async_copy(some, some, sem).wait()


def combine(parts):
    peak = jnp.max(parts, axis=0)
    return peak + jnp.log2(jnp.sum(jnp.exp2(parts - peak[None]), axis=0))


def spread(potential, wide, first):
    for q in range(potential.shape[0]):
        block = jnp.broadcast_to(potential[q : q + 1, :], (LANES, LANES))
        wide[pl.ds(pl.multiple_of(first + q * LANES, LANES), LANES), :] = block.T


def online(peak, total, z):
    z = z.reshape(z.shape[0] // 8, 8, LANES)
    top = jnp.maximum(peak, jnp.max(z, axis=0))
    return top, total * jnp.exp2(peak - top) + jnp.sum(jnp.exp2(z - top[None]), axis=0)


def accumulate(scores, wide, first, count, lane_col, width, state):
    def step(r, state):
        rows = pl.ds(pl.multiple_of(first + r * ROWS_AT_ONCE, ROWS_AT_ONCE), ROWS_AT_ONCE)
        add = wide[rows, :]
        done = []
        for q in range(width):
            cols = pl.ds((lane_col + q) * LANES, LANES)
            done.append(online(*state[q], scores[rows, cols] + add))
        return tuple(done)

    steps = count // ROWS_AT_ONCE
    return lax.fori_loop(0, steps, step, state, unroll=min(max(8, 64 // width), steps))


def fresh(width):
    low = jnp.full((8, LANES), LOWEST, jnp.float32)
    return ((low, jnp.zeros((8, LANES), jnp.float32)),) * width


def finish(peak, total):
    top = jnp.max(peak, axis=0, keepdims=True)
    return top + jnp.log2(jnp.sum(total * jnp.exp2(peak - top), axis=0, keepdims=True))


def cut(cuts, blocks):
    unit = blocks // sum(cuts) if blocks >= sum(cuts) else 0
    widths = [c * unit for c in cuts] if unit else [blocks // 2, blocks // 2]
    return [(sum(widths[:k]), width) for k, width in enumerate(widths)]


def kernel(nr, nc, s_in, t_in, g_in, f_out, g_out, *scratch):
    scratch = list(scratch)
    s_all, t_all, s_cat, t_cat, s_rows, t_rows, w, wt, p_wide, q_wide, s_sq, t_sq, g_now, p_now = scratch[:14]
    local, s_sem, t_send, t_recv, p_sem, q_sem = scratch[14:20]
    src_chunks, tgt_chunks = cut(SRC_CUTS, nc), cut(TGT_CUTS, nr)
    p_parts = scratch[20 : 20 + len(src_chunks)]
    q_parts = scratch[20 + len(src_chunks) :]
    row, col = lax.axis_index("rows"), lax.axis_index("cols")
    in_rows = ring_partners(row, nr)
    in_cols = torus_partners(col, nc)
    n_src, n_tgt = nc * LANES, nr * LANES
    bits_src = math.log2(n_src * nr)
    bits_tgt = math.log2(n_tgt * nc)

    barrier = pltpu.get_barrier_semaphore()
    for axis, partners in (("rows", in_rows), ("cols", in_cols)):
        for partner in partners:
            pl.semaphore_signal(barrier, inc=1, device_id={axis: partner}, device_id_type=MESH)
    staged = [
        pltpu.make_async_copy(t_in, t_all.at[row], local.at[0]),
        pltpu.make_async_copy(s_in, s_all.at[col], local.at[1]),
        pltpu.make_async_copy(g_in, g_now, local.at[2]),
    ]
    for copy in staged:
        copy.start()
    for copy in staged:
        copy.wait()
    pl.semaphore_wait(barrier, len(in_rows) + len(in_cols))

    core = lax.rem(row, 2)
    sibling = row + 1 - 2 * core
    chips = nr // 2

    def far_row(step):
        return lax.rem(row + 2 * step, nr)

    def target_copy(shard, to, send_sem):
        return pltpu.make_async_remote_copy(
            src_ref=t_all.at[shard],
            dst_ref=t_all.at[shard],
            send_sem=send_sem,
            recv_sem=t_recv.at[shard],
            device_id={"rows": to},
            device_id_type=MESH,
        )

    by_distance = sorted(range(1, chips), key=lambda k: min(k, chips - k))
    for step in reversed(by_distance):
        target_copy(row, far_row(step), t_send.at[0]).start()
    here = s_all.at[col]
    send_to_all(here, here, s_sem.at[0], s_sem.at[1], "cols", in_cols)
    target_copy(row, sibling, t_send.at[1]).start()
    for step in by_distance:
        shard = far_row(step)
        target_copy(shard, sibling, t_send.at[1]).wait_recv()
        target_copy(shard, sibling, t_send.at[1]).start()
    empty = jnp.zeros((DEPTH - 6 * 32, LANES), jnp.bfloat16)

    def lay(points, scale, order, cat, turned, sq, q):
        x = points[q]
        sq[pl.ds(q, 1), :] = jnp.sum(x * x, axis=0, keepdims=True)
        pieces = split3(x * scale)
        block = jnp.concatenate([pieces[k] for k in order] + [empty], axis=0)
        at = pl.ds(pl.multiple_of(q * LANES, LANES), LANES)
        cat[:, at] = block
        if turned is not None:
            turned[at, :] = block.T

    wait_for_all(s_all, s_sem.at[1])

    @pl.loop(0, nc)
    def _(q):
        lay(s_all, 1.0, (0, 0, 1, 1, 0, 2), s_cat, None, s_sq, q)

    def lay_target(shard):
        lay(t_all, 2.0 * TO_BITS, (0, 1, 0, 1, 2, 0), t_cat, t_rows, t_sq, shard)
        start = (g_now[pl.ds(shard, 1), :] - t_sq[pl.ds(shard, 1), :]) * TO_BITS
        spread(start, q_wide, shard * LANES)

    def nearest(k):
        away = lax.div(k + 1, 2)
        return lax.rem(row + 2 * (chips + (2 * lax.rem(k, 2) - 1) * away), nr)

    @pl.loop(0, chips)
    def _(k):
        lay_target(nearest(k))

    @pl.loop(0, chips)
    def _(k):
        shard = nearest(k) + 1 - 2 * core
        target_copy(shard, sibling, t_send.at[1]).wait_recv()
        lay_target(shard)

    def products(left, right, out):
        tile = min(512, right.shape[1])

        @pl.loop(0, right.shape[1] // tile)
        def _(c):
            cols = pl.ds(pl.multiple_of(c * tile, tile), tile)
            out[:, cols] = jnp.dot(left[...], right[:, cols], preferred_element_type=jnp.float32)

    for c, (first, width) in enumerate(src_chunks):

        @pl.loop(0, width // 2)
        def _(t):
            cols = pl.ds(pl.multiple_of((first + 2 * t) * LANES, 2 * LANES), 2 * LANES)

            def step(r, state):
                rows = pl.ds(pl.multiple_of(r * LANES, LANES), LANES)
                both = jnp.dot(t_rows[rows, :], s_cat[:, cols], preferred_element_type=jnp.float32)
                add = q_wide[rows, :]
                return tuple(online(*state[q], both[:, q * LANES : (q + 1) * LANES] + add) for q in range(2))

            state = lax.fori_loop(0, nr, step, fresh(2), unroll=True)
            for q in range(2):
                p_parts[c][0, col, pl.ds(2 * t + q, 1), :] = finish(*state[q])

        here = p_parts[c].at[0, col]
        send_to_all(here, here, p_sem.at[0, 0, c], p_sem.at[1, 0, c], "cols", in_cols)


    def take_target(it, d):
        first, width = tgt_chunks[d]
        wait_for_all(q_parts[d].at[it], q_sem.at[0, it, d])
        wait_for_all(q_parts[d].at[it], q_sem.at[1, it, d])
        q = bits_src - combine(q_parts[d][it])
        g_now[first : first + width, :] = q
        return q

    def row_pass(it):
        for c, (first, width) in enumerate(src_chunks):
            state = fresh(width)
            if c == 0:
                for d, (lane_col, cols) in enumerate(tgt_chunks):
                    spread(take_target(it - 1, d), q_wide, lane_col * LANES)
                    state = accumulate(wt, q_wide, lane_col * LANES, cols * LANES, first, width, state)
            else:
                state = accumulate(wt, q_wide, 0, n_tgt, first, width, state)
            for q in range(width):
                p_parts[c][it, col, q : q + 1, :] = finish(*state[q])
            here = p_parts[c].at[it, col]
            send_to_all(here, here, p_sem.at[0, it, c], p_sem.at[1, it, c], "cols", in_cols)

    @pl.loop(0, ITERS)
    def _(it):
        @pl.when(it == 0)
        def _():
            for q in range(nc):
                at = pl.ds(q * LANES, LANES)
                s_rows[at, :] = s_cat[:, at].T
            products(s_rows, t_cat, w)
            wait_for_all(s_all, s_sem.at[0])
            some = t_all.at[pl.ds(0, chips - 1)]
            pltpu.make_async_copy(some, some, t_send.at[0]).wait()
            some = t_all.at[pl.ds(0, chips)]
            pltpu.make_async_copy(some, some, t_send.at[1]).wait()

        whole = fresh(nr)
        for c, (first, width) in enumerate(src_chunks):
            wait_for_all(p_parts[c].at[it], p_sem.at[0, it, c])
            wait_for_all(p_parts[c].at[it], p_sem.at[1, it, c])
            p = bits_tgt - combine(p_parts[c][it])
            p_now[first : first + width, :] = p
            start, depth = first * LANES, width * LANES
            spread(p, p_wide, start)
            if c < len(src_chunks) - 1:
                whole = accumulate(w, p_wide, start, depth, 0, nr, whole)
                continue
            for d, (lane_col, cols) in enumerate(tgt_chunks):
                state = accumulate(w, p_wide, start, depth, lane_col, cols, whole[lane_col : lane_col + cols])
                for q in range(cols):
                    q_parts[d][it, row, q : q + 1, :] = finish(*state[q])
                here = q_parts[d].at[it, row]
                send_to_all(here, here, q_sem.at[0, it, d], q_sem.at[1, it, d], "rows", in_rows)

        @pl.when(it == 0)
        def _():
            products(t_rows, s_cat, wt)

        @pl.when(it < ITERS - 1)
        def _():
            row_pass(it + 1)

    for d in range(len(tgt_chunks)):
        take_target(ITERS - 1, d)
    f_out[...] = s_sq[...] + FROM_BITS * p_now[...]
    g_out[...] = t_sq[...] + FROM_BITS * g_now[...]


def hand_over(f_ref, g_ref, f_out, g_out):
    f_out[...] = f_ref[...]
    g_out[...] = g_ref[...]


def body(source_points, target_points, target_init):
    nr, nc = lax.axis_size("rows"), lax.axis_size("cols")
    n_src, n_tgt = nc * LANES, nr * LANES
    f32, bf16 = jnp.float32, jnp.bfloat16
    src_chunks, tgt_chunks = cut(SRC_CUTS, nc), cut(TGT_CUTS, nr)
    f, g = pl.pallas_call(
        functools.partial(kernel, nr, nc),
        out_shape=(jax.ShapeDtypeStruct((nc, LANES), f32), jax.ShapeDtypeStruct((nr, LANES), f32)),
        in_specs=[pl.BlockSpec(memory_space=pl.ANY)] * 3,
        out_specs=[pl.BlockSpec(memory_space=pltpu.VMEM)] * 2,
        scratch_shapes=[
            pltpu.VMEM((nc,) + source_points.shape, f32),
            pltpu.VMEM((nr,) + target_points.shape, f32),
            pltpu.VMEM((DEPTH, n_src), bf16),
            pltpu.VMEM((DEPTH, n_tgt), bf16),
            pltpu.VMEM((n_src, DEPTH), bf16),
            pltpu.VMEM((n_tgt, DEPTH), bf16),
            pltpu.VMEM((n_src, n_tgt), f32),
            pltpu.VMEM((n_tgt, n_src), f32),
            pltpu.VMEM((n_src, LANES), f32),
            pltpu.VMEM((n_tgt, LANES), f32),
            pltpu.VMEM((nc, LANES), f32),
            pltpu.VMEM((nr, LANES), f32),
            pltpu.VMEM((nr, LANES), f32),
            pltpu.VMEM((nc, LANES), f32),
            pltpu.SemaphoreType.DMA((3,)),
            pltpu.SemaphoreType.DMA((2,)),
            pltpu.SemaphoreType.DMA((2,)),
            pltpu.SemaphoreType.DMA((nr,)),
            pltpu.SemaphoreType.DMA((2, ITERS, len(src_chunks))),
            pltpu.SemaphoreType.DMA((2, ITERS, len(tgt_chunks))),
        ]
        + [pltpu.VMEM((ITERS, nc, width, LANES), f32) for _, width in src_chunks]
        + [pltpu.VMEM((ITERS, nr, width, LANES), f32) for _, width in tgt_chunks],
        compiler_params=pltpu.CompilerParams(
            collective_id=0, has_side_effects=True, vmem_limit_bytes=56 << 20
        ),
        name="sinkhorn",
    )(source_points, target_points, target_init.reshape(nr, LANES))
    f, g = pl.pallas_call(
        hand_over,
        out_shape=(jax.ShapeDtypeStruct((nc, LANES), f32), jax.ShapeDtypeStruct((nr, LANES), f32)),
        in_specs=[pl.BlockSpec(memory_space=pltpu.VMEM)] * 2,
        out_specs=[pl.BlockSpec(memory_space=pltpu.VMEM)] * 2,
        name="hand_over",
    )(f, g)
    return f.reshape(-1), g.reshape(-1)


def solution(mesh):
    in_specs = (P(None, ("rows", "cols")), P(None, ("cols", "rows")), P("cols"))
    out_specs = (P("rows"), P("cols"))
    return jax.shard_map(body, mesh=mesh, in_specs=in_specs, out_specs=out_specs, check_vma=False)
```

```python
import functools
import math

import jax
import jax.numpy as jnp
from jax import lax
from jax.experimental import pallas as pl
from jax.experimental.pallas import tpu as pltpu
from jax.sharding import PartitionSpec as P

ITERS = 4
EPS = 0.2
SRC_CUTS = (8, 8)
TGT_CUTS = (8, 8)
LANES = 128
ROWS_AT_ONCE = 64
DEPTH = 256
LOWEST = -1e30
TO_BITS = 1.0 / (EPS * math.log(2.0))
FROM_BITS = EPS * math.log(2.0)
MESH = pl.DeviceIdType.MESH


def ring_partners(me, size):
    steps = sorted(range(1, size), key=lambda k: -min(k // 2, (size - k) // 2))
    return [lax.rem(me + k, size) for k in steps]


def torus_partners(me, size):
    side = math.isqrt(size)
    x, y = lax.div(me, side), lax.rem(me, side)
    moves = [(a, b) for a in range(side) for b in range(side) if a + b > 0]
    moves.sort(key=lambda m: -(min(m[0], side - m[0]) + min(m[1], side - m[1])))
    return [lax.rem(x + a, side) * side + lax.rem(y + b, side) for a, b in moves]


def split3(x):
    hi = x.astype(jnp.bfloat16)
    rest = x - hi.astype(jnp.float32)
    mid = rest.astype(jnp.bfloat16)
    low = (rest - mid.astype(jnp.float32)).astype(jnp.bfloat16)
    return hi, mid, low


def send_to_all(src, dst, send_sem, recv_sem, axis, partners):
    for partner in partners:
        pltpu.make_async_remote_copy(
            src_ref=src,
            dst_ref=dst,
            send_sem=send_sem,
            recv_sem=recv_sem,
            device_id={axis: partner},
            device_id_type=MESH,
        ).start()


def wait_for_all(slots, sem):
    some = slots.at[pl.ds(0, slots.shape[0] - 1)]
    pltpu.make_async_copy(some, some, sem).wait()


def combine(parts):
    peak = jnp.max(parts, axis=0)
    return peak + jnp.log2(jnp.sum(jnp.exp2(parts - peak[None]), axis=0))


def spread(potential, wide, first):
    for q in range(potential.shape[0]):
        block = jnp.broadcast_to(potential[q : q + 1, :], (LANES, LANES))
        wide[pl.ds(pl.multiple_of(first + q * LANES, LANES), LANES), :] = block.T


def online(peak, total, z):
    z = z.reshape(z.shape[0] // 8, 8, LANES)
    top = jnp.maximum(peak, jnp.max(z, axis=0))
    return top, total * jnp.exp2(peak - top) + jnp.sum(jnp.exp2(z - top[None]), axis=0)


def accumulate(scores, wide, first, count, lane_col, width, state):
    def step(r, state):
        rows = pl.ds(pl.multiple_of(first + r * ROWS_AT_ONCE, ROWS_AT_ONCE), ROWS_AT_ONCE)
        add = wide[rows, :]
        done = []
        for q in range(width):
            cols = pl.ds((lane_col + q) * LANES, LANES)
            done.append(online(*state[q], scores[rows, cols] + add))
        return tuple(done)

    steps = count // ROWS_AT_ONCE
    return lax.fori_loop(0, steps, step, state, unroll=min(max(8, 64 // width), steps))


def fresh(width):
    low = jnp.full((8, LANES), LOWEST, jnp.float32)
    return ((low, jnp.zeros((8, LANES), jnp.float32)),) * width


def finish(peak, total):
    top = jnp.max(peak, axis=0, keepdims=True)
    return top + jnp.log2(jnp.sum(total * jnp.exp2(peak - top), axis=0, keepdims=True))


def cut(cuts, blocks):
    unit = blocks // sum(cuts) if blocks >= sum(cuts) else 0
    widths = [c * unit for c in cuts] if unit else [blocks // 2, blocks // 2]
    return [(sum(widths[:k]), width) for k, width in enumerate(widths)]


def kernel(nr, nc, s_in, t_in, g_in, f_out, g_out, *scratch):
    scratch = list(scratch)
    s_all, t_all, s_cat, t_cat, s_rows, t_rows, w, wt, p_wide, q_wide, s_sq, t_sq, g_now, p_now = scratch[:14]
    local, s_sem, t_send, t_recv, p_sem, q_sem = scratch[14:20]
    src_chunks, tgt_chunks = cut(SRC_CUTS, nc), cut(TGT_CUTS, nr)
    p_parts = scratch[20 : 20 + len(src_chunks)]
    q_parts = scratch[20 + len(src_chunks) :]
    row, col = lax.axis_index("rows"), lax.axis_index("cols")
    in_rows = ring_partners(row, nr)
    in_cols = torus_partners(col, nc)
    n_src, n_tgt = nc * LANES, nr * LANES
    bits_src = math.log2(n_src * nr)
    bits_tgt = math.log2(n_tgt * nc)

    barrier = pltpu.get_barrier_semaphore()
    for axis, partners in (("rows", in_rows), ("cols", in_cols)):
        for partner in partners:
            pl.semaphore_signal(barrier, inc=1, device_id={axis: partner}, device_id_type=MESH)
    staged = [
        pltpu.make_async_copy(t_in, t_all.at[row], local.at[0]),
        pltpu.make_async_copy(s_in, s_all.at[col], local.at[1]),
        pltpu.make_async_copy(g_in, g_now, local.at[2]),
    ]
    for copy in staged:
        copy.start()
    for copy in staged:
        copy.wait()
    pl.semaphore_wait(barrier, len(in_rows) + len(in_cols))

    core = lax.rem(row, 2)
    sibling = row + 1 - 2 * core
    chips = nr // 2

    def far_row(step):
        return lax.rem(row + 2 * step, nr)

    def target_copy(shard, to, send_sem):
        return pltpu.make_async_remote_copy(
            src_ref=t_all.at[shard],
            dst_ref=t_all.at[shard],
            send_sem=send_sem,
            recv_sem=t_recv.at[shard],
            device_id={"rows": to},
            device_id_type=MESH,
        )

    by_distance = sorted(range(1, chips), key=lambda k: min(k, chips - k))
    for step in reversed(by_distance):
        target_copy(row, far_row(step), t_send.at[0]).start()
    here = s_all.at[col]
    send_to_all(here, here, s_sem.at[0], s_sem.at[1], "cols", in_cols)
    target_copy(row, sibling, t_send.at[1]).start()
    for step in by_distance:
        shard = far_row(step)
        target_copy(shard, sibling, t_send.at[1]).wait_recv()
        target_copy(shard, sibling, t_send.at[1]).start()
    empty = jnp.zeros((DEPTH - 6 * 32, LANES), jnp.bfloat16)

    def lay(points, scale, order, cat, turned, sq, q):
        x = points[q]
        sq[pl.ds(q, 1), :] = jnp.sum(x * x, axis=0, keepdims=True)
        pieces = split3(x * scale)
        block = jnp.concatenate([pieces[k] for k in order] + [empty], axis=0)
        at = pl.ds(pl.multiple_of(q * LANES, LANES), LANES)
        cat[:, at] = block
        if turned is not None:
            turned[at, :] = block.T

    wait_for_all(s_all, s_sem.at[1])

    @pl.loop(0, nc, unroll=4)
    def _(q):
        lay(s_all, 1.0, (0, 0, 1, 1, 0, 2), s_cat, None, s_sq, q)

    def lay_target(shard):
        lay(t_all, 2.0 * TO_BITS, (0, 1, 0, 1, 2, 0), t_cat, t_rows, t_sq, shard)
        start = (g_now[pl.ds(shard, 1), :] - t_sq[pl.ds(shard, 1), :]) * TO_BITS
        spread(start, q_wide, shard * LANES)

    def nearest(k):
        away = lax.div(k + 1, 2)
        return lax.rem(row + 2 * (chips + (2 * lax.rem(k, 2) - 1) * away), nr)

    @pl.loop(0, chips, unroll=min(4, chips))
    def _(k):
        lay_target(nearest(k))

    @pl.loop(0, chips)
    def _(k):
        shard = nearest(k) + 1 - 2 * core
        target_copy(shard, sibling, t_send.at[1]).wait_recv()
        lay_target(shard)

    def products(left, right, out):
        tile = min(512, right.shape[1])

        @pl.loop(0, right.shape[1] // tile)
        def _(c):
            cols = pl.ds(pl.multiple_of(c * tile, tile), tile)
            out[:, cols] = jnp.dot(left[...], right[:, cols], preferred_element_type=jnp.float32)

    for c, (first, width) in enumerate(src_chunks):

        @pl.loop(0, width // 2)
        def _(t):
            cols = pl.ds(pl.multiple_of((first + 2 * t) * LANES, 2 * LANES), 2 * LANES)

            def step(r, state):
                rows = pl.ds(pl.multiple_of(r * LANES, LANES), LANES)
                both = jnp.dot(t_rows[rows, :], s_cat[:, cols], preferred_element_type=jnp.float32)
                add = q_wide[rows, :]
                return tuple(online(*state[q], both[:, q * LANES : (q + 1) * LANES] + add) for q in range(2))

            state = lax.fori_loop(0, nr, step, fresh(2), unroll=True)
            for q in range(2):
                p_parts[c][0, col, pl.ds(2 * t + q, 1), :] = finish(*state[q])

        here = p_parts[c].at[0, col]
        send_to_all(here, here, p_sem.at[0, 0, c], p_sem.at[1, 0, c], "cols", in_cols)


    def take_target(it, d):
        first, width = tgt_chunks[d]
        wait_for_all(q_parts[d].at[it], q_sem.at[0, it, d])
        wait_for_all(q_parts[d].at[it], q_sem.at[1, it, d])
        q = bits_src - combine(q_parts[d][it])
        g_now[first : first + width, :] = q
        return q

    def row_pass(it):
        for c, (first, width) in enumerate(src_chunks):
            state = fresh(width)
            if c == 0:
                for d, (lane_col, cols) in enumerate(tgt_chunks):
                    spread(take_target(it - 1, d), q_wide, lane_col * LANES)
                    state = accumulate(wt, q_wide, lane_col * LANES, cols * LANES, first, width, state)
            else:
                state = accumulate(wt, q_wide, 0, n_tgt, first, width, state)
            for q in range(width):
                p_parts[c][it, col, q : q + 1, :] = finish(*state[q])
            here = p_parts[c].at[it, col]
            send_to_all(here, here, p_sem.at[0, it, c], p_sem.at[1, it, c], "cols", in_cols)

    @pl.loop(0, ITERS)
    def _(it):
        @pl.when(it == 0)
        def _():
            for q in range(nc):
                at = pl.ds(q * LANES, LANES)
                s_rows[at, :] = s_cat[:, at].T
            products(s_rows, t_cat, w)
            wait_for_all(s_all, s_sem.at[0])
            some = t_all.at[pl.ds(0, chips - 1)]
            pltpu.make_async_copy(some, some, t_send.at[0]).wait()
            some = t_all.at[pl.ds(0, chips)]
            pltpu.make_async_copy(some, some, t_send.at[1]).wait()

        whole = fresh(nr)
        for c, (first, width) in enumerate(src_chunks):
            wait_for_all(p_parts[c].at[it], p_sem.at[0, it, c])
            wait_for_all(p_parts[c].at[it], p_sem.at[1, it, c])
            p = bits_tgt - combine(p_parts[c][it])
            p_now[first : first + width, :] = p
            start, depth = first * LANES, width * LANES
            spread(p, p_wide, start)
            if c < len(src_chunks) - 1:
                whole = accumulate(w, p_wide, start, depth, 0, nr, whole)
                continue
            for d, (lane_col, cols) in enumerate(tgt_chunks):
                state = accumulate(w, p_wide, start, depth, lane_col, cols, whole[lane_col : lane_col + cols])
                for q in range(cols):
                    q_parts[d][it, row, q : q + 1, :] = finish(*state[q])
                here = q_parts[d].at[it, row]
                send_to_all(here, here, q_sem.at[0, it, d], q_sem.at[1, it, d], "rows", in_rows)

        @pl.when(it == 0)
        def _():
            products(t_rows, s_cat, wt)

        @pl.when(it < ITERS - 1)
        def _():
            row_pass(it + 1)

    for d in range(len(tgt_chunks)):
        take_target(ITERS - 1, d)
    f_out[...] = s_sq[...] + FROM_BITS * p_now[...]
    g_out[...] = t_sq[...] + FROM_BITS * g_now[...]


def hand_over(f_ref, g_ref, f_out, g_out):
    f_out[...] = f_ref[...]
    g_out[...] = g_ref[...]


def body(source_points, target_points, target_init):
    nr, nc = lax.axis_size("rows"), lax.axis_size("cols")
    n_src, n_tgt = nc * LANES, nr * LANES
    f32, bf16 = jnp.float32, jnp.bfloat16
    src_chunks, tgt_chunks = cut(SRC_CUTS, nc), cut(TGT_CUTS, nr)
    f, g = pl.pallas_call(
        functools.partial(kernel, nr, nc),
        out_shape=(jax.ShapeDtypeStruct((nc, LANES), f32), jax.ShapeDtypeStruct((nr, LANES), f32)),
        in_specs=[pl.BlockSpec(memory_space=pl.ANY)] * 3,
        out_specs=[pl.BlockSpec(memory_space=pltpu.VMEM)] * 2,
        scratch_shapes=[
            pltpu.VMEM((nc,) + source_points.shape, f32),
            pltpu.VMEM((nr,) + target_points.shape, f32),
            pltpu.VMEM((DEPTH, n_src), bf16),
            pltpu.VMEM((DEPTH, n_tgt), bf16),
            pltpu.VMEM((n_src, DEPTH), bf16),
            pltpu.VMEM((n_tgt, DEPTH), bf16),
            pltpu.VMEM((n_src, n_tgt), f32),
            pltpu.VMEM((n_tgt, n_src), f32),
            pltpu.VMEM((n_src, LANES), f32),
            pltpu.VMEM((n_tgt, LANES), f32),
            pltpu.VMEM((nc, LANES), f32),
            pltpu.VMEM((nr, LANES), f32),
            pltpu.VMEM((nr, LANES), f32),
            pltpu.VMEM((nc, LANES), f32),
            pltpu.SemaphoreType.DMA((3,)),
            pltpu.SemaphoreType.DMA((2,)),
            pltpu.SemaphoreType.DMA((2,)),
            pltpu.SemaphoreType.DMA((nr,)),
            pltpu.SemaphoreType.DMA((2, ITERS, len(src_chunks))),
            pltpu.SemaphoreType.DMA((2, ITERS, len(tgt_chunks))),
        ]
        + [pltpu.VMEM((ITERS, nc, width, LANES), f32) for _, width in src_chunks]
        + [pltpu.VMEM((ITERS, nr, width, LANES), f32) for _, width in tgt_chunks],
        compiler_params=pltpu.CompilerParams(
            collective_id=0, has_side_effects=True, vmem_limit_bytes=56 << 20
        ),
        name="sinkhorn",
    )(source_points, target_points, target_init.reshape(nr, LANES))
    f, g = pl.pallas_call(
        hand_over,
        out_shape=(jax.ShapeDtypeStruct((nc, LANES), f32), jax.ShapeDtypeStruct((nr, LANES), f32)),
        in_specs=[pl.BlockSpec(memory_space=pltpu.VMEM)] * 2,
        out_specs=[pl.BlockSpec(memory_space=pltpu.VMEM)] * 2,
        name="hand_over",
    )(f, g)
    return f.reshape(-1), g.reshape(-1)


def solution(mesh):
    in_specs = (P(None, ("rows", "cols")), P(None, ("cols", "rows")), P("cols"))
    out_specs = (P("rows"), P("cols"))
    return jax.shard_map(body, mesh=mesh, in_specs=in_specs, out_specs=out_specs, check_vma=False)
```

```python
import functools
import math

import jax
import jax.numpy as jnp
from jax import lax
from jax.experimental import pallas as pl
from jax.experimental.pallas import tpu as pltpu
from jax.sharding import PartitionSpec as P

ITERS = 4
EPS = 0.2
SRC_CUTS = (8, 8)
TGT_CUTS = (8, 8)
LANES = 128
ROWS_AT_ONCE = 64
DEPTH = 256
LOWEST = -1e30
TO_BITS = 1.0 / (EPS * math.log(2.0))
FROM_BITS = EPS * math.log(2.0)
MESH = pl.DeviceIdType.MESH


def ring_partners(me, size):
    steps = sorted(range(1, size), key=lambda k: -min(k // 2, (size - k) // 2))
    return [lax.rem(me + k, size) for k in steps]


def torus_partners(me, size):
    side = math.isqrt(size)
    x, y = lax.div(me, side), lax.rem(me, side)
    moves = [(a, b) for a in range(side) for b in range(side) if a + b > 0]
    moves.sort(key=lambda m: -(min(m[0], side - m[0]) + min(m[1], side - m[1])))
    return [lax.rem(x + a, side) * side + lax.rem(y + b, side) for a, b in moves]


def split3(x):
    hi = x.astype(jnp.bfloat16)
    rest = x - hi.astype(jnp.float32)
    mid = rest.astype(jnp.bfloat16)
    low = (rest - mid.astype(jnp.float32)).astype(jnp.bfloat16)
    return hi, mid, low


def send_to_all(src, dst, send_sem, recv_sem, axis, partners):
    for partner in partners:
        pltpu.make_async_remote_copy(
            src_ref=src,
            dst_ref=dst,
            send_sem=send_sem,
            recv_sem=recv_sem,
            device_id={axis: partner},
            device_id_type=MESH,
        ).start()


def wait_for_all(slots, sem):
    some = slots.at[pl.ds(0, slots.shape[0] - 1)]
    pltpu.make_async_copy(some, some, sem).wait()


def combine(parts):
    peak = jnp.max(parts, axis=0)
    return peak + jnp.log2(jnp.sum(jnp.exp2(parts - peak[None]), axis=0))


def spread(potential, wide, first):
    for q in range(potential.shape[0]):
        block = jnp.broadcast_to(potential[q : q + 1, :], (LANES, LANES))
        wide[pl.ds(pl.multiple_of(first + q * LANES, LANES), LANES), :] = block.T


def online(peak, total, z):
    z = z.reshape(z.shape[0] // 8, 8, LANES)
    top = jnp.maximum(peak, jnp.max(z, axis=0))
    return top, total * jnp.exp2(peak - top) + jnp.sum(jnp.exp2(z - top[None]), axis=0)


def accumulate(scores, wide, first, count, lane_col, width, state):
    def step(r, state):
        rows = pl.ds(pl.multiple_of(first + r * ROWS_AT_ONCE, ROWS_AT_ONCE), ROWS_AT_ONCE)
        add = wide[rows, :]
        done = []
        for q in range(width):
            cols = pl.ds((lane_col + q) * LANES, LANES)
            done.append(online(*state[q], scores[rows, cols] + add))
        return tuple(done)

    steps = count // ROWS_AT_ONCE
    return lax.fori_loop(0, steps, step, state, unroll=min(max(8, 64 // width), steps))


def fresh(width):
    low = jnp.full((8, LANES), LOWEST, jnp.float32)
    return ((low, jnp.zeros((8, LANES), jnp.float32)),) * width


def finish(peak, total):
    top = jnp.max(peak, axis=0, keepdims=True)
    return top + jnp.log2(jnp.sum(total * jnp.exp2(peak - top), axis=0, keepdims=True))


def cut(cuts, blocks):
    unit = blocks // sum(cuts) if blocks >= sum(cuts) else 0
    widths = [c * unit for c in cuts] if unit else [blocks // 2, blocks // 2]
    return [(sum(widths[:k]), width) for k, width in enumerate(widths)]


def kernel(nr, nc, s_in, t_in, g_in, f_out, g_out, *scratch):
    scratch = list(scratch)
    s_all, t_all, s_cat, t_cat, s_rows, t_rows, w, wt, p_wide, q_wide, s_sq, t_sq, g_now, p_now = scratch[:14]
    local, s_sem, t_send, t_recv, p_sem, q_sem = scratch[14:20]
    src_chunks, tgt_chunks = cut(SRC_CUTS, nc), cut(TGT_CUTS, nr)
    p_parts = scratch[20 : 20 + len(src_chunks)]
    q_parts = scratch[20 + len(src_chunks) :]
    row, col = lax.axis_index("rows"), lax.axis_index("cols")
    in_rows = ring_partners(row, nr)
    in_cols = torus_partners(col, nc)
    n_src, n_tgt = nc * LANES, nr * LANES
    bits_src = math.log2(n_src * nr)
    bits_tgt = math.log2(n_tgt * nc)

    barrier = pltpu.get_barrier_semaphore()
    for axis, partners in (("rows", in_rows), ("cols", in_cols)):
        for partner in partners:
            pl.semaphore_signal(barrier, inc=1, device_id={axis: partner}, device_id_type=MESH)
    staged = [
        pltpu.make_async_copy(t_in, t_all.at[row], local.at[0]),
        pltpu.make_async_copy(s_in, s_all.at[col], local.at[1]),
        pltpu.make_async_copy(g_in, g_now, local.at[2]),
    ]
    for copy in staged:
        copy.start()
    for copy in staged:
        copy.wait()
    pl.semaphore_wait(barrier, len(in_rows) + len(in_cols))

    core = lax.rem(row, 2)
    sibling = row + 1 - 2 * core
    chips = nr // 2

    def far_row(step):
        return lax.rem(row + 2 * step, nr)

    def target_copy(shard, to, send_sem):
        return pltpu.make_async_remote_copy(
            src_ref=t_all.at[shard],
            dst_ref=t_all.at[shard],
            send_sem=send_sem,
            recv_sem=t_recv.at[shard],
            device_id={"rows": to},
            device_id_type=MESH,
        )

    by_distance = sorted(range(1, chips), key=lambda k: min(k, chips - k))
    for step in reversed(by_distance):
        target_copy(row, far_row(step), t_send.at[0]).start()
    here = s_all.at[col]
    send_to_all(here, here, s_sem.at[0], s_sem.at[1], "cols", in_cols)
    target_copy(row, sibling, t_send.at[1]).start()
    for step in by_distance:
        shard = far_row(step)
        target_copy(shard, sibling, t_send.at[1]).wait_recv()
        target_copy(shard, sibling, t_send.at[1]).start()
    empty = jnp.zeros((DEPTH - 6 * 32, LANES), jnp.bfloat16)

    def lay(points, scale, order, cat, turned, sq, q):
        x = points[q]
        sq[pl.ds(q, 1), :] = jnp.sum(x * x, axis=0, keepdims=True)
        pieces = split3(x * scale)
        block = jnp.concatenate([pieces[k] for k in order] + [empty], axis=0)
        at = pl.ds(pl.multiple_of(q * LANES, LANES), LANES)
        cat[:, at] = block
        if turned is not None:
            turned[at, :] = block.T

    wait_for_all(s_all, s_sem.at[1])

    @pl.loop(0, nc, unroll=4)
    def _(q):
        lay(s_all, 1.0, (0, 0, 1, 1, 0, 2), s_cat, None, s_sq, q)

    def lay_target(shard):
        lay(t_all, 2.0 * TO_BITS, (0, 1, 0, 1, 2, 0), t_cat, t_rows, t_sq, shard)
        start = (g_now[pl.ds(shard, 1), :] - t_sq[pl.ds(shard, 1), :]) * TO_BITS
        spread(start, q_wide, shard * LANES)

    def nearest(k):
        away = lax.div(k + 1, 2)
        return lax.rem(row + 2 * (chips + (2 * lax.rem(k, 2) - 1) * away), nr)

    @pl.loop(0, chips, unroll=min(4, chips))
    def _(k):
        lay_target(nearest(k))

    @pl.loop(0, chips)
    def _(k):
        target_copy(nearest(k) + 1 - 2 * core, sibling, t_send.at[1]).wait_recv()

    @pl.loop(0, chips, unroll=min(4, chips))
    def _(k):
        lay_target(nearest(k) + 1 - 2 * core)

    def products(left, right, out):
        tile = min(512, right.shape[1])

        @pl.loop(0, right.shape[1] // tile)
        def _(c):
            cols = pl.ds(pl.multiple_of(c * tile, tile), tile)
            out[:, cols] = jnp.dot(left[...], right[:, cols], preferred_element_type=jnp.float32)

    for c, (first, width) in enumerate(src_chunks):

        @pl.loop(0, width // 2)
        def _(t):
            cols = pl.ds(pl.multiple_of((first + 2 * t) * LANES, 2 * LANES), 2 * LANES)

            def step(r, state):
                rows = pl.ds(pl.multiple_of(r * LANES, LANES), LANES)
                both = jnp.dot(t_rows[rows, :], s_cat[:, cols], preferred_element_type=jnp.float32)
                add = q_wide[rows, :]
                return tuple(online(*state[q], both[:, q * LANES : (q + 1) * LANES] + add) for q in range(2))

            state = lax.fori_loop(0, nr, step, fresh(2), unroll=True)
            for q in range(2):
                p_parts[c][0, col, pl.ds(2 * t + q, 1), :] = finish(*state[q])

        here = p_parts[c].at[0, col]
        send_to_all(here, here, p_sem.at[0, 0, c], p_sem.at[1, 0, c], "cols", in_cols)


    def take_target(it, d):
        first, width = tgt_chunks[d]
        wait_for_all(q_parts[d].at[it], q_sem.at[0, it, d])
        wait_for_all(q_parts[d].at[it], q_sem.at[1, it, d])
        q = bits_src - combine(q_parts[d][it])
        g_now[first : first + width, :] = q
        return q

    def row_pass(it):
        for c, (first, width) in enumerate(src_chunks):
            state = fresh(width)
            if c == 0:
                for d, (lane_col, cols) in enumerate(tgt_chunks):
                    spread(take_target(it - 1, d), q_wide, lane_col * LANES)
                    state = accumulate(wt, q_wide, lane_col * LANES, cols * LANES, first, width, state)
            else:
                state = accumulate(wt, q_wide, 0, n_tgt, first, width, state)
            for q in range(width):
                p_parts[c][it, col, q : q + 1, :] = finish(*state[q])
            here = p_parts[c].at[it, col]
            send_to_all(here, here, p_sem.at[0, it, c], p_sem.at[1, it, c], "cols", in_cols)

    @pl.loop(0, ITERS)
    def _(it):
        @pl.when(it == 0)
        def _():
            for q in range(nc):
                at = pl.ds(q * LANES, LANES)
                s_rows[at, :] = s_cat[:, at].T
            products(s_rows, t_cat, w)
            wait_for_all(s_all, s_sem.at[0])
            some = t_all.at[pl.ds(0, chips - 1)]
            pltpu.make_async_copy(some, some, t_send.at[0]).wait()
            some = t_all.at[pl.ds(0, chips)]
            pltpu.make_async_copy(some, some, t_send.at[1]).wait()

        whole = fresh(nr)
        for c, (first, width) in enumerate(src_chunks):
            wait_for_all(p_parts[c].at[it], p_sem.at[0, it, c])
            wait_for_all(p_parts[c].at[it], p_sem.at[1, it, c])
            p = bits_tgt - combine(p_parts[c][it])
            p_now[first : first + width, :] = p
            start, depth = first * LANES, width * LANES
            spread(p, p_wide, start)
            if c < len(src_chunks) - 1:
                whole = accumulate(w, p_wide, start, depth, 0, nr, whole)
                continue
            for d, (lane_col, cols) in enumerate(tgt_chunks):
                state = accumulate(w, p_wide, start, depth, lane_col, cols, whole[lane_col : lane_col + cols])
                for q in range(cols):
                    q_parts[d][it, row, q : q + 1, :] = finish(*state[q])
                here = q_parts[d].at[it, row]
                send_to_all(here, here, q_sem.at[0, it, d], q_sem.at[1, it, d], "rows", in_rows)

        @pl.when(it == 0)
        def _():
            products(t_rows, s_cat, wt)

        @pl.when(it < ITERS - 1)
        def _():
            row_pass(it + 1)

    for d in range(len(tgt_chunks)):
        take_target(ITERS - 1, d)
    f_out[...] = s_sq[...] + FROM_BITS * p_now[...]
    g_out[...] = t_sq[...] + FROM_BITS * g_now[...]


def hand_over(f_ref, g_ref, f_out, g_out):
    f_out[...] = f_ref[...]
    g_out[...] = g_ref[...]


def body(source_points, target_points, target_init):
    nr, nc = lax.axis_size("rows"), lax.axis_size("cols")
    n_src, n_tgt = nc * LANES, nr * LANES
    f32, bf16 = jnp.float32, jnp.bfloat16
    src_chunks, tgt_chunks = cut(SRC_CUTS, nc), cut(TGT_CUTS, nr)
    f, g = pl.pallas_call(
        functools.partial(kernel, nr, nc),
        out_shape=(jax.ShapeDtypeStruct((nc, LANES), f32), jax.ShapeDtypeStruct((nr, LANES), f32)),
        in_specs=[pl.BlockSpec(memory_space=pl.ANY)] * 3,
        out_specs=[pl.BlockSpec(memory_space=pltpu.VMEM)] * 2,
        scratch_shapes=[
            pltpu.VMEM((nc,) + source_points.shape, f32),
            pltpu.VMEM((nr,) + target_points.shape, f32),
            pltpu.VMEM((DEPTH, n_src), bf16),
            pltpu.VMEM((DEPTH, n_tgt), bf16),
            pltpu.VMEM((n_src, DEPTH), bf16),
            pltpu.VMEM((n_tgt, DEPTH), bf16),
            pltpu.VMEM((n_src, n_tgt), f32),
            pltpu.VMEM((n_tgt, n_src), f32),
            pltpu.VMEM((n_src, LANES), f32),
            pltpu.VMEM((n_tgt, LANES), f32),
            pltpu.VMEM((nc, LANES), f32),
            pltpu.VMEM((nr, LANES), f32),
            pltpu.VMEM((nr, LANES), f32),
            pltpu.VMEM((nc, LANES), f32),
            pltpu.SemaphoreType.DMA((3,)),
            pltpu.SemaphoreType.DMA((2,)),
            pltpu.SemaphoreType.DMA((2,)),
            pltpu.SemaphoreType.DMA((nr,)),
            pltpu.SemaphoreType.DMA((2, ITERS, len(src_chunks))),
            pltpu.SemaphoreType.DMA((2, ITERS, len(tgt_chunks))),
        ]
        + [pltpu.VMEM((ITERS, nc, width, LANES), f32) for _, width in src_chunks]
        + [pltpu.VMEM((ITERS, nr, width, LANES), f32) for _, width in tgt_chunks],
        compiler_params=pltpu.CompilerParams(
            collective_id=0, has_side_effects=True, vmem_limit_bytes=56 << 20
        ),
        name="sinkhorn",
    )(source_points, target_points, target_init.reshape(nr, LANES))
    f, g = pl.pallas_call(
        hand_over,
        out_shape=(jax.ShapeDtypeStruct((nc, LANES), f32), jax.ShapeDtypeStruct((nr, LANES), f32)),
        in_specs=[pl.BlockSpec(memory_space=pltpu.VMEM)] * 2,
        out_specs=[pl.BlockSpec(memory_space=pltpu.VMEM)] * 2,
        name="hand_over",
    )(f, g)
    return f.reshape(-1), g.reshape(-1)


def solution(mesh):
    in_specs = (P(None, ("rows", "cols")), P(None, ("cols", "rows")), P("cols"))
    out_specs = (P("rows"), P("cols"))
    return jax.shard_map(body, mesh=mesh, in_specs=in_specs, out_specs=out_specs, check_vma=False)
```
